32 devices in a mesh: row: 8 (over z, x), col: 4 (over y, core).
Axes of the slice: x: 2, y: 2, z: 4, core: 2. Of those that a mesh axis runs over, the one named last changes fastest.
Arguments:
- gradient: bfloat16 [8192, 28672], P('row', 'col'), may hold values from -6 to 6
- projector: bfloat16 [8192, 1024], P('row'), may hold values from -0.25 to 0.25
- first_moment: float32 [1024, 28672], P('row', 'col'), may hold values from -6 to 6
- second_moment: float32 [1024, 28672], P('row', 'col'), may hold values from 5e-05 to 0.12, as said below
Outputs:
- update: bfloat16 [8192, 28672], P('row', 'col')
- first_new: float32 [1024, 28672], P('row', 'col')
- second_new: float32 [1024, 28672], P('row', 'col')
The draws below stay inside these ranges and needn't reach their ends.
Inputs may be any that keep to these rules, and one draw needn't show every extreme that they name: `second_moment`: entries are positive.
All inputs are finite; a program needn't handle non-finite values.
Results may differ from the reference program's by a relative error of at most 0.038.
Values may be sent and summed in bfloat16 or wider, within the bound.
A program may use at most 128 MiB of HBM per device.

```python
import math
import jax
import jax.numpy as jnp
from jax import lax

D = 8192
FF = 28672
R = 1024
N_ROW = 8


def draw_second_moment(key, part):
    key_base = jax.random.fold_in(key, 11)
    key_column = jax.random.fold_in(key, 12)
    position = jnp.arange(R, dtype=jnp.float32)[:, None] / R
    column_place = jnp.arange(FF, dtype=jnp.float32)[None, :] / FF
    column_noise = jax.random.uniform(key_column, (1, FF), jnp.float32, 0.0, 1.0)
    base = jax.random.uniform(key_base, (R, FF), jnp.float32, 0.5, 2.0)
    return 0.0001 * base * jnp.exp(math.log(10.0) * (position + 0.5 * column_place + 0.5 * column_noise))


def spiked(entries, key, source, target, parts, factor):
    def block_of(axis_at):
        return (jnp.arange(entries.shape[axis_at]) // (entries.shape[axis_at] // parts)).reshape((-1,) + (1,) * (entries.ndim - 1 - axis_at))

    first = jax.random.permutation(key, parts)[block_of(target)]
    second = (block_of(target) + parts // 2) % parts
    return jnp.where((block_of(source) == first) | (block_of(source) == second), factor * entries, entries)


def levels(stream_key, extent, pieces, least, largest):
    factor_of, own = 1.0, jax.random.fold_in(stream_key, 6)
    for dim, parts in pieces:
        heights = jnp.exp(jax.random.uniform(jax.random.fold_in(own, dim), (parts,), jnp.float32, least / len(pieces), largest / len(pieces)))
        factor_of = factor_of * jnp.repeat(heights, extent[dim] // parts).reshape([-1 if axis == dim else 1 for axis in range(len(extent))])
    return factor_of


def gaussian(own_key, extent, spread, limit, split=(), held_as=jnp.bfloat16):
    factor_of = levels(own_key, extent, split, -0.22, 0.18) if split else 1.0
    drawn = jax.random.normal(own_key, extent, jnp.float32) * spread * factor_of
    return jnp.minimum(jnp.maximum(drawn, -limit), limit).astype(held_as)


def bell_draw_with(stream_key, extent, spread, bound, shards, heavy, kind=jnp.bfloat16):
    drawn = spread * jax.random.normal(stream_key, extent, jnp.float32)
    if shards:
        drawn = drawn * levels(stream_key, extent, shards, -0.22, 0.18)
    return jnp.clip(spiked(drawn, jax.random.fold_in(stream_key, 3), *heavy), -bound, bound).astype(kind)


def setup_inputs(seed: int = 0) -> dict:
    key_list = jax.random.split(jax.random.key(seed), 5)
    return {
        "gradient": gaussian(key_list[0], (D, FF), 1.0, 6.0, ((0, 8), (1, 4))),
        "projector": bell_draw_with(key_list[1], (D, R), R ** -0.5, 0.25, ((0, 8),), (0, 1, 8, 2.0)),
        "first_moment": gaussian(key_list[2], (R, FF), 1.0, 6.0, ((0, 8), (1, 4)), jnp.float32),
        "second_moment": draw_second_moment(jax.random.fold_in(key_list[4], 71), 0),
    }


decay_first = 0.9
decay_second = 0.999
bias_first = 1.0 - 0.9 ** 10
bias_second = 1.0 - 0.999 ** 10
epsilon = 1e-08
clip_limit = 0.5

def reference(gradient, projector, first_moment, second_moment):
    block_rows = D // N_ROW

    def block_term(index, running):
        offset = (index * block_rows).astype(jnp.int32)
        basis_block = lax.dynamic_slice_in_dim(projector, offset, block_rows, 0)
        grad_block = lax.dynamic_slice_in_dim(gradient, offset, block_rows, 0)
        product = lax.dot_general(basis_block, grad_block, (((0,), (0,)), ((), ())), preferred_element_type=jnp.float32)
        rounded = lax.optimization_barrier(product.astype(jnp.bfloat16))
        return running + rounded.astype(jnp.float32)
    lowrank = lax.fori_loop(0, N_ROW, block_term, jnp.zeros((R, FF), jnp.float32))
    first_new = decay_first * first_moment + (1.0 - decay_first) * lowrank
    second_new = decay_second * second_moment + (1.0 - decay_second) * lowrank * lowrank
    direction = first_new / bias_first / (jnp.sqrt(second_new / bias_second) + epsilon)
    root_mean = jnp.sqrt(jnp.sum(direction * direction) / (R * FF) + 1e-06)
    factor = jnp.minimum(1.0, clip_limit / root_mean)
    step_low = (factor * direction).astype(jnp.bfloat16)
    update = jnp.dot(projector, step_low, preferred_element_type=jnp.float32).astype(jnp.bfloat16)
    return (update, first_new, second_new)
```

```python
import functools
import itertools

import jax
import jax.numpy as jnp
from jax import lax
from jax.experimental import pallas as pl
from jax.experimental.pallas import tpu as pltpu
from jax.sharding import PartitionSpec as P

MESH = pl.DeviceIdType.MESH

decay_first = 0.9
decay_second = 0.999
bias_first = 1.0 - 0.9**10
bias_second = 1.0 - 0.999**10
epsilon = 1e-08
clip_limit = 0.5

CHUNKS = 14
LEAD = 2
VMEM_BYTES = 60 * 1024 * 1024


def log2(count):
    return count.bit_length() - 1


def orders(m):
    plain = tuple(range(m))
    if m < 2:
        return plain, plain
    return plain, (1, 0) + plain[2:]


def kernel(n_row, n_col, chunks, pt_ref, g_ref, m1_ref, m2_ref, *rest):
    m, mc = log2(n_row), log2(n_col)
    gath, f_ref, s_ref, sq_ref, part, gbuf, dirv, acc, slots = rest[:9]
    recvs = rest[9 : 9 + m]
    gsem, rs_send, rs_recv, ag_send, ag_recv, loc, sq_send, sq_recv = rest[9 + m :]
    rb, w = part.shape[-2:]
    rank = pt_ref.shape[0]

    def bits_of(axis, count):
        me = lax.axis_index(axis)
        mine = [(me // (1 << b)) % 2 for b in range(count)]
        return mine, [{axis: me + (1 << b) * (1 - 2 * mine[b])} for b in range(count)]

    mine, partner = bits_of("row", m)
    _, col_partner = bits_of("col", mc)
    everyone = partner + col_partner

    def cols(c):
        return pl.ds(pl.multiple_of(c * w, w), w)

    def load(c):
        return pltpu.make_async_copy(g_ref.at[:, cols(c)], gbuf.at[c % 2], gsem.at[c % 2])

    load(0).start()
    barrier = pltpu.get_barrier_semaphore()
    for device in everyone:
        pl.semaphore_signal(barrier, inc=1, device_id=device, device_id_type=MESH)
    pl.semaphore_wait(barrier, len(everyone))
    acc[0] = jnp.zeros(acc.shape[1:], acc.dtype)

    def index(fixed):
        return tuple(fixed.get(b, slice(None)) for b in reversed(range(m)))

    def rs_copy(c, j, order):
        fixed = {b: mine[b] for b in order[:j]}
        fixed[order[j]] = 1 - mine[order[j]]
        return pltpu.make_async_remote_copy(
            src_ref=part.at[(c,) + index(fixed)],
            dst_ref=recvs[j].at[c],
            send_sem=rs_send.at[j, c],
            recv_sem=rs_recv.at[j, c],
            device_id=partner[order[j]],
            device_id_type=MESH,
        )

    def ag_copy(c, j, order):
        fixed = {b: mine[b] for b in order[: m - j]}
        view = gath.at[index(fixed) + (slice(None), cols(c))]
        return pltpu.make_async_remote_copy(
            src_ref=dirv.at[c] if j == 0 else view,
            dst_ref=view,
            send_sem=ag_send.at[j, c],
            recv_sem=ag_recv.at[j, c],
            device_id=partner[order[m - 1 - j]],
            device_id_type=MESH,
        )

    def own_copy(c):
        view = gath.at[index(dict(enumerate(mine))) + (slice(None), cols(c))]
        return pltpu.make_async_copy(dirv.at[c], view, loc.at[c])

    def project(c):
        @pl.when(c + 1 < chunks)
        def _():
            load(c + 1).start()

        load(c).wait()
        tile = min(256, rank)
        per = tile // rb

        @pl.loop(0, rank // tile)
        def _(i):
            rows = pl.ds(pl.multiple_of(i * tile, tile), tile)
            product = jnp.dot(pt_ref[rows, :], gbuf[c % 2], preferred_element_type=jnp.float32)
            product = product.astype(part.dtype)
            for k in range(per):
                owner = i * per + k
                where = tuple((owner // (1 << b)) % 2 for b in reversed(range(m)))
                part[(c,) + where] = product[k * rb : (k + 1) * rb]

    def add(c, j, order):
        fixed = {b: mine[b] for b in order[: j + 1]}
        free = [b for b in reversed(range(m)) if b not in fixed]
        for values in itertools.product(range(2), repeat=len(free)):
            at = (c,) + index({**fixed, **dict(zip(free, values))})
            arrived = recvs[j][(c,) + values].astype(jnp.float32)
            part[at] = (part[at].astype(jnp.float32) + arrived).astype(part.dtype)

    def adam(c):
        at = (c,) + index(dict(enumerate(mine)))
        step = min(32, rb)
        for r in range(0, rb, step):
            rows = pl.ds(r, step)
            low = part[at + (rows, slice(None))].astype(jnp.float32)
            low = low + recvs[m - 1][c, rows, :].astype(jnp.float32)
            first = decay_first * m1_ref[rows, cols(c)] + (1.0 - decay_first) * low
            second = decay_second * m2_ref[rows, cols(c)] + (1.0 - decay_second) * low * low
            f_ref[rows, cols(c)] = first
            s_ref[rows, cols(c)] = second
            direction = first / bias_first / (jnp.sqrt(second / bias_second) + epsilon)
            dirv[c, rows, :] = direction.astype(dirv.dtype)
            square = direction * direction
            total = square[0:8]
            for k in range(8, step, 8):
                total = total + square[k : k + 8]
            for k in range(0, w, 128):
                acc[0] += total[:, k : k + 128]

    last = 2 * m

    def step(c, s):
        for kind, order in enumerate(orders(m)):

            @pl.when((c >= 0) & (c < chunks) & ((c % 4 == 3) == (kind == 1)))
            def _():
                if 0 < s <= m:
                    rs_copy(c, s - 1, order).wait_recv()
                if s == 0:
                    project(c)
                elif s < m:
                    add(c, s - 1, order)
                elif s == m:
                    adam(c)
                    own_copy(c).start()
                else:
                    ag_copy(c, s - m - 1, order).wait_recv()
                    if s == m + 1:
                        own_copy(c).wait()
                if s < m:
                    rs_copy(c, s, order).start()
                elif s < last:
                    ag_copy(c, s - m, order).start()

    def tick(t, steps):
        for s in steps:
            step(t - (LEAD + s if s else 0), s)

    def square_copy(i):
        return pltpu.make_async_remote_copy(
            src_ref=acc.at[i],
            dst_ref=slots.at[i],
            send_sem=sq_send.at[i],
            recv_sem=sq_recv.at[i],
            device_id=everyone[i],
            device_id_type=MESH,
        )

    def square_step(i):
        square_copy(i).wait_recv()
        acc[i + 1] = acc[i] + slots[i]
        if i + 1 < len(everyone):
            square_copy(i + 1).start()

    done = chunks + LEAD + m

    @pl.loop(0, done)
    def _(t):
        tick(t, range(last, -1, -1))

    square_copy(0).start()
    at = 0
    for k in range(m):
        until = len(everyone) * (k + 1) // m
        while at < until:
            square_step(at)
            at += 1
        for s in range(last, m + k, -1):
            step(jnp.int32(done + k - LEAD - s), s)
    sq_ref[...] = acc[len(everyone)]

    for i in range(len(everyone)):
        square_copy(i).wait_send()

    @pl.loop(0, chunks)
    def _(c):
        for kind, order in enumerate(orders(m)):

            @pl.when((c % 4 == 3) == (kind == 1))
            def _():
                for j in range(m):
                    rs_copy(c, j, order).wait_send()
                    ag_copy(c, j, order).wait_send()


def local(n_row, n_col, gradient, projector, first_moment, second_moment):
    m, mc = log2(n_row), log2(n_col)
    rows, width = gradient.shape
    rank = projector.shape[1]
    rb, w = rank // n_row, width // CHUNKS
    bf16, f32 = jnp.bfloat16, jnp.float32
    pairs = (2,) * m
    whole = pl.BlockSpec(memory_space=pltpu.VMEM)
    hbm = pl.BlockSpec(memory_space=pl.ANY)
    links = m + mc
    gathered, first_new, second_new, squares = pl.pallas_call(
        functools.partial(kernel, n_row, n_col, CHUNKS),
        out_shape=[
            jax.ShapeDtypeStruct(pairs + (rb, width), bf16),
            jax.ShapeDtypeStruct((rb, width), f32),
            jax.ShapeDtypeStruct((rb, width), f32),
            jax.ShapeDtypeStruct((8, 128), f32),
        ],
        in_specs=[whole, hbm, whole, whole],
        out_specs=[hbm, whole, whole, whole],
        scratch_shapes=[
            pltpu.VMEM((CHUNKS,) + pairs + (rb, w), bf16),
            pltpu.VMEM((2, rows, w), bf16),
            pltpu.VMEM((CHUNKS, rb, w), bf16),
            pltpu.VMEM((links + 1, 8, 128), f32),
            pltpu.VMEM((links, 8, 128), f32),
        ]
        + [pltpu.VMEM((CHUNKS,) + pairs[j + 1 :] + (rb, w), bf16) for j in range(m)]
        + [pltpu.SemaphoreType.DMA((2,))]
        + [pltpu.SemaphoreType.DMA((m, CHUNKS))] * 4
        + [pltpu.SemaphoreType.DMA((CHUNKS,))]
        + [pltpu.SemaphoreType.DMA((links,))] * 2,
        cost_estimate=pl.CostEstimate(
            flops=2 * rows * rank * width,
            bytes_accessed=2 * rows * width + 2 * rank * width + 16 * rb * width,
            transcendentals=rb * width,
        ),
        compiler_params=pltpu.CompilerParams(
            collective_id=0, has_side_effects=True, vmem_limit_bytes=VMEM_BYTES
        ),
    )(projector.T, gradient, first_moment, second_moment)
    entries = rank * width * n_col
    root_mean = jnp.sqrt(jnp.sum(squares) / entries + 1e-06)
    factor = jnp.minimum(1.0, clip_limit / root_mean)
    projected = jnp.dot(
        projector, gathered.reshape(rank, width), preferred_element_type=jnp.float32
    )
    return ((projected * factor).astype(bf16), first_new, second_new)


def solution(mesh):
    placed = (P("row", "col"), P("row", None), P("row", "col"), P("row", "col"))
    return jax.shard_map(
        functools.partial(local, mesh.shape["row"], mesh.shape["col"]),
        mesh=mesh,
        in_specs=placed,
        out_specs=(P("row", "col"), P("row", "col"), P("row", "col")),
        check_vma=False,
    )
```

```python
import functools
import itertools

import jax
import jax.numpy as jnp
from jax import lax
from jax.experimental import pallas as pl
from jax.experimental.pallas import tpu as pltpu
from jax.sharding import PartitionSpec as P

MESH = pl.DeviceIdType.MESH

decay_first = 0.9
decay_second = 0.999
bias_first = 1.0 - 0.9**10
bias_second = 1.0 - 0.999**10
epsilon = 1e-08
clip_limit = 0.5

LEAD = 3
VMEM_BYTES = 60 * 1024 * 1024


def chunks_of(width):
    return next(k for k in (28, 14, 8, 7, 4, 2, 1) if width % (128 * k) == 0 or k == 1)


def log2(count):
    return count.bit_length() - 1


def orders(m):
    plain = tuple(range(m))
    if m < 2:
        return plain, plain
    return plain, (1, 0) + plain[2:]


def kernel(n_row, n_col, chunks, pt_ref, g_ref, m1_ref, m2_ref, *rest):
    m, mc = log2(n_row), log2(n_col)
    gath, f_ref, s_ref, sq_ref, part, gbuf, dirv, acc, slots = rest[:9]
    recvs = rest[9 : 9 + m]
    gsem, rs_send, rs_recv, ag_send, ag_recv, loc, sq_send, sq_recv = rest[9 + m :]
    rb, w = part.shape[-2:]
    rank = pt_ref.shape[0]

    def bits_of(axis, count):
        me = lax.axis_index(axis)
        mine = [(me // (1 << b)) % 2 for b in range(count)]
        return mine, [{axis: me + (1 << b) * (1 - 2 * mine[b])} for b in range(count)]

    mine, partner = bits_of("row", m)
    _, col_partner = bits_of("col", mc)
    everyone = partner + col_partner

    def cols(c):
        return pl.ds(pl.multiple_of(c * w, w), w)

    def load(c):
        return pltpu.make_async_copy(g_ref.at[:, cols(c)], gbuf.at[c % 2], gsem.at[c % 2])

    load(0).start()
    barrier = pltpu.get_barrier_semaphore()
    for device in everyone:
        pl.semaphore_signal(barrier, inc=1, device_id=device, device_id_type=MESH)
    pl.semaphore_wait(barrier, len(everyone))
    acc[0] = jnp.zeros(acc.shape[1:], acc.dtype)

    def index(fixed):
        return tuple(fixed.get(b, slice(None)) for b in reversed(range(m)))

    def rs_copy(c, j, order):
        fixed = {b: mine[b] for b in order[:j]}
        fixed[order[j]] = 1 - mine[order[j]]
        return pltpu.make_async_remote_copy(
            src_ref=part.at[(c,) + index(fixed)],
            dst_ref=recvs[j].at[c],
            send_sem=rs_send.at[j, c],
            recv_sem=rs_recv.at[j, c],
            device_id=partner[order[j]],
            device_id_type=MESH,
        )

    def ag_copy(c, j, order):
        fixed = {b: mine[b] for b in order[: m - j]}
        view = gath.at[index(fixed) + (slice(None), cols(c))]
        return pltpu.make_async_remote_copy(
            src_ref=dirv.at[c] if j == 0 else view,
            dst_ref=view,
            send_sem=ag_send.at[j, c],
            recv_sem=ag_recv.at[j, c],
            device_id=partner[order[m - 1 - j]],
            device_id_type=MESH,
        )

    def own_copy(c):
        view = gath.at[index(dict(enumerate(mine))) + (slice(None), cols(c))]
        return pltpu.make_async_copy(dirv.at[c], view, loc.at[c])

    def project(c):
        @pl.when(c + 1 < chunks)
        def _():
            load(c + 1).start()

        load(c).wait()
        tile = min(256, rank)
        per = tile // rb

        @pl.loop(0, rank // tile)
        def _(i):
            rows = pl.ds(pl.multiple_of(i * tile, tile), tile)
            product = jnp.dot(pt_ref[rows, :], gbuf[c % 2], preferred_element_type=jnp.float32)
            product = product.astype(part.dtype)
            for k in range(per):
                owner = i * per + k
                where = tuple((owner // (1 << b)) % 2 for b in reversed(range(m)))
                part[(c,) + where] = product[k * rb : (k + 1) * rb]

    def add(c, j, order):
        fixed = {b: mine[b] for b in order[: j + 1]}
        free = [b for b in reversed(range(m)) if b not in fixed]
        for values in itertools.product(range(2), repeat=len(free)):
            at = (c,) + index({**fixed, **dict(zip(free, values))})
            arrived = recvs[j][(c,) + values].astype(jnp.float32)
            part[at] = (part[at].astype(jnp.float32) + arrived).astype(part.dtype)

    def adam(c):
        at = (c,) + index(dict(enumerate(mine)))
        step = min(32, rb)
        for r in range(0, rb, step):
            rows = pl.ds(r, step)
            low = part[at + (rows, slice(None))].astype(jnp.float32)
            low = low + recvs[m - 1][c, rows, :].astype(jnp.float32)
            first = decay_first * m1_ref[rows, cols(c)] + (1.0 - decay_first) * low
            second = decay_second * m2_ref[rows, cols(c)] + (1.0 - decay_second) * low * low
            f_ref[rows, cols(c)] = first
            s_ref[rows, cols(c)] = second
            direction = first / bias_first / (jnp.sqrt(second / bias_second) + epsilon)
            dirv[c, rows, :] = direction.astype(dirv.dtype)
            square = direction * direction
            total = square[0:8]
            for k in range(8, step, 8):
                total = total + square[k : k + 8]
            for k in range(0, w, 128):
                acc[0] += total[:, k : k + 128]

    last = 2 * m

    def step(c, s):
        for kind, order in enumerate(orders(m)):

            @pl.when((c >= 0) & (c < chunks) & ((c % 4 == 3) == (kind == 1)))
            def _():
                if 0 < s <= m:
                    rs_copy(c, s - 1, order).wait_recv()
                if s == 0:
                    project(c)
                elif s < m:
                    add(c, s - 1, order)
                elif s == m:
                    adam(c)
                    own_copy(c).start()
                else:
                    ag_copy(c, s - m - 1, order).wait_recv()
                    if s == m + 1:
                        own_copy(c).wait()
                if s < m:
                    rs_copy(c, s, order).start()
                elif s < last:
                    ag_copy(c, s - m, order).start()

    def tick(t, steps):
        for s in steps:
            step(t - (LEAD + s if s else 0), s)

    def square_copy(i):
        return pltpu.make_async_remote_copy(
            src_ref=acc.at[i],
            dst_ref=slots.at[i],
            send_sem=sq_send.at[i],
            recv_sem=sq_recv.at[i],
            device_id=everyone[i],
            device_id_type=MESH,
        )

    def square_step(i):
        square_copy(i).wait_recv()
        acc[i + 1] = acc[i] + slots[i]
        if i + 1 < len(everyone):
            square_copy(i + 1).start()

    done = chunks + LEAD + m

    @pl.loop(0, done)
    def _(t):
        tick(t, range(last, -1, -1))

    square_copy(0).start()
    at = 0
    for k in range(m):
        until = len(everyone) * (k + 1) // m
        while at < until:
            square_step(at)
            at += 1
        for s in range(last, m + k, -1):
            step(jnp.int32(done + k - LEAD - s), s)
    sq_ref[...] = acc[len(everyone)]

    for i in range(len(everyone)):
        square_copy(i).wait_send()

    @pl.loop(0, chunks)
    def _(c):
        for kind, order in enumerate(orders(m)):

            @pl.when((c % 4 == 3) == (kind == 1))
            def _():
                for j in range(m):
                    rs_copy(c, j, order).wait_send()
                    ag_copy(c, j, order).wait_send()


def local(n_row, n_col, gradient, projector, first_moment, second_moment):
    m, mc = log2(n_row), log2(n_col)
    rows, width = gradient.shape
    rank = projector.shape[1]
    chunks = chunks_of(width)
    rb, w = rank // n_row, width // chunks
    bf16, f32 = jnp.bfloat16, jnp.float32
    pairs = (2,) * m
    whole = pl.BlockSpec(memory_space=pltpu.VMEM)
    hbm = pl.BlockSpec(memory_space=pl.ANY)
    links = m + mc
    gathered, first_new, second_new, squares = pl.pallas_call(
        functools.partial(kernel, n_row, n_col, chunks),
        out_shape=[
            jax.ShapeDtypeStruct(pairs + (rb, width), bf16),
            jax.ShapeDtypeStruct((rb, width), f32),
            jax.ShapeDtypeStruct((rb, width), f32),
            jax.ShapeDtypeStruct((8, 128), f32),
        ],
        in_specs=[whole, hbm, whole, whole],
        out_specs=[hbm, whole, whole, whole],
        scratch_shapes=[
            pltpu.VMEM((chunks,) + pairs + (rb, w), bf16),
            pltpu.VMEM((2, rows, w), bf16),
            pltpu.VMEM((chunks, rb, w), bf16),
            pltpu.VMEM((links + 1, 8, 128), f32),
            pltpu.VMEM((links, 8, 128), f32),
        ]
        + [pltpu.VMEM((chunks,) + pairs[j + 1 :] + (rb, w), bf16) for j in range(m)]
        + [pltpu.SemaphoreType.DMA((2,))]
        + [pltpu.SemaphoreType.DMA((m, chunks))] * 4
        + [pltpu.SemaphoreType.DMA((chunks,))]
        + [pltpu.SemaphoreType.DMA((links,))] * 2,
        cost_estimate=pl.CostEstimate(
            flops=2 * rows * rank * width,
            bytes_accessed=2 * rows * width + 2 * rank * width + 16 * rb * width,
            transcendentals=rb * width,
        ),
        compiler_params=pltpu.CompilerParams(
            collective_id=0, has_side_effects=True, vmem_limit_bytes=VMEM_BYTES
        ),
    )(projector.T, gradient, first_moment, second_moment)
    return back_project(n_col, projector, gathered.reshape(rank, width), squares, first_new, second_new)


def back_kernel(entries, p_ref, d_ref, sq_ref, f_ref, s_ref, u_ref, fo_ref, so_ref):
    root_mean = jnp.sqrt(jnp.sum(sq_ref[...], keepdims=True) / entries + 1e-06)
    factor = jnp.minimum(1.0, clip_limit / root_mean)
    rows = p_ref.shape[0]
    tile = min(256, rows)
    for r in range(0, rows, tile):
        projected = jnp.dot(p_ref[r : r + tile, :], d_ref[...], preferred_element_type=jnp.float32)
        u_ref[r : r + tile, :] = (projected * factor).astype(u_ref.dtype)
    fo_ref[...] = f_ref[...]
    so_ref[...] = s_ref[...]


def back_project(n_col, projector, gathered, squares, first_new, second_new):
    rows, rank = projector.shape
    width = gathered.shape[1]
    rb = first_new.shape[0]
    steps = next(k for k in (14, 8, 7, 4, 2, 1) if width % (128 * k) == 0 or k == 1)
    w = width // steps

    def across(height):
        return pl.BlockSpec((height, w), lambda i: (0, i))

    def fixed(shape):
        return pl.BlockSpec(shape, lambda i: (0, 0))

    return pl.pallas_call(
        functools.partial(back_kernel, rank * width * n_col),
        grid=(steps,),
        out_shape=[
            jax.ShapeDtypeStruct((rows, width), jnp.bfloat16),
            jax.ShapeDtypeStruct((rb, width), jnp.float32),
            jax.ShapeDtypeStruct((rb, width), jnp.float32),
        ],
        in_specs=[fixed((rows, rank)), across(rank), fixed((8, 128)), across(rb), across(rb)],
        out_specs=[across(rows), across(rb), across(rb)],
        compiler_params=pltpu.CompilerParams(vmem_limit_bytes=40 * 1024 * 1024),
    )(projector, gathered, squares, first_new, second_new)


def solution(mesh):
    placed = (P("row", "col"), P("row", None), P("row", "col"), P("row", "col"))
    return jax.shard_map(
        functools.partial(local, mesh.shape["row"], mesh.shape["col"]),
        mesh=mesh,
        in_specs=placed,
        out_specs=(P("row", "col"), P("row", "col"), P("row", "col")),
        check_vma=False,
    )
```

```python
import functools
import itertools

import jax
import jax.numpy as jnp
from jax import lax
from jax.experimental import pallas as pl
from jax.experimental.pallas import tpu as pltpu
from jax.sharding import PartitionSpec as P

MESH = pl.DeviceIdType.MESH

decay_first = 0.9
decay_second = 0.999
bias_first = 1.0 - 0.9**10
bias_second = 1.0 - 0.999**10
epsilon = 1e-08
clip_limit = 0.5

LEAD = 2
STRIDE = 2
VMEM_BYTES = 60 * 1024 * 1024


def chunks_of(width):
    return next(k for k in (28, 14, 8, 7, 4, 2, 1) if width % (128 * k) == 0 or k == 1)


def log2(count):
    return count.bit_length() - 1


def orders(m):
    plain = tuple(range(m))
    if m < 2:
        return plain, plain
    return plain, (1, 0) + plain[2:]


def kernel(n_row, n_col, chunks, p_ref, g_ref, m1_ref, m2_ref, *rest):
    m, mc = log2(n_row), log2(n_col)
    gath, f_ref, s_ref, sq_ref, u_ref, part, gbuf, dirv, acc, slots, pt_ref, dbuf, ubuf = rest[:13]
    recvs = rest[13 : 13 + m]
    gsem, dsem, usem, rs_send, rs_recv, ag_send, ag_recv, loc, sq_send, sq_recv = rest[13 + m :]
    rb, w = part.shape[-2:]
    rows_here, rank = p_ref.shape

    def bits_of(axis, count):
        me = lax.axis_index(axis)
        mine = [(me // (1 << b)) % 2 for b in range(count)]
        return mine, [{axis: me + (1 << b) * (1 - 2 * mine[b])} for b in range(count)]

    mine, partner = bits_of("row", m)
    _, col_partner = bits_of("col", mc)
    everyone = partner + col_partner

    def cols(c):
        return pl.ds(pl.multiple_of(c * w, w), w)

    def load(c):
        return pltpu.make_async_copy(g_ref.at[:, cols(c)], gbuf.at[c % 2], gsem.at[c % 2])

    load(0).start()
    for r in range(0, rank, min(256, rank)):
        pt_ref[r : r + min(256, rank), :] = p_ref[:, r : r + min(256, rank)].T
    barrier = pltpu.get_barrier_semaphore()
    for device in everyone:
        pl.semaphore_signal(barrier, inc=1, device_id=device, device_id_type=MESH)
    pl.semaphore_wait(barrier, len(everyone))
    acc[0] = jnp.zeros(acc.shape[1:], acc.dtype)

    def index(fixed):
        return tuple(fixed.get(b, slice(None)) for b in reversed(range(m)))

    def rs_copy(c, j, order):
        fixed = {b: mine[b] for b in order[:j]}
        fixed[order[j]] = 1 - mine[order[j]]
        return pltpu.make_async_remote_copy(
            src_ref=part.at[(c,) + index(fixed)],
            dst_ref=recvs[j].at[c],
            send_sem=rs_send.at[j, c],
            recv_sem=rs_recv.at[j, c],
            device_id=partner[order[j]],
            device_id_type=MESH,
        )

    def ag_copy(c, j, order):
        fixed = {b: mine[b] for b in order[: m - j]}
        view = gath.at[index(fixed) + (slice(None), cols(c))]
        return pltpu.make_async_remote_copy(
            src_ref=dirv.at[c] if j == 0 else view,
            dst_ref=view,
            send_sem=ag_send.at[j, c],
            recv_sem=ag_recv.at[j, c],
            device_id=partner[order[m - 1 - j]],
            device_id_type=MESH,
        )

    def own_copy(c):
        view = gath.at[index(dict(enumerate(mine))) + (slice(None), cols(c))]
        return pltpu.make_async_copy(dirv.at[c], view, loc.at[c])

    def project(c):
        @pl.when(c + 1 < chunks)
        def _():
            load(c + 1).start()

        load(c).wait()
        tile = min(256, rank)
        per = tile // rb

        @pl.loop(0, rank // tile)
        def _(i):
            rows = pl.ds(pl.multiple_of(i * tile, tile), tile)
            product = jnp.dot(pt_ref[rows, :], gbuf[c % 2], preferred_element_type=jnp.float32)
            product = product.astype(part.dtype)
            for k in range(per):
                owner = i * per + k
                where = tuple((owner // (1 << b)) % 2 for b in reversed(range(m)))
                part[(c,) + where] = product[k * rb : (k + 1) * rb]

    def add(c, j, order):
        fixed = {b: mine[b] for b in order[: j + 1]}
        free = [b for b in reversed(range(m)) if b not in fixed]
        for values in itertools.product(range(2), repeat=len(free)):
            at = (c,) + index({**fixed, **dict(zip(free, values))})
            arrived = recvs[j][(c,) + values].astype(jnp.float32)
            part[at] = (part[at].astype(jnp.float32) + arrived).astype(part.dtype)

    def adam(c):
        at = (c,) + index(dict(enumerate(mine)))
        step = min(32, rb)
        for r in range(0, rb, step):
            rows = pl.ds(r, step)
            low = part[at + (rows, slice(None))].astype(jnp.float32)
            low = low + recvs[m - 1][c, rows, :].astype(jnp.float32)
            first = decay_first * m1_ref[rows, cols(c)] + (1.0 - decay_first) * low
            second = decay_second * m2_ref[rows, cols(c)] + (1.0 - decay_second) * low * low
            f_ref[rows, cols(c)] = first
            s_ref[rows, cols(c)] = second
            direction = first / bias_first / (jnp.sqrt(second / bias_second) + epsilon)
            dirv[c, rows, :] = direction.astype(dirv.dtype)
            square = direction * direction
            total = square[0:8]
            for k in range(8, step, 8):
                total = total + square[k : k + 8]
            for k in range(0, w, 128):
                acc[0] += total[:, k : k + 128]

    def gathered_load(c):
        return pltpu.make_async_copy(
            gath.at[(slice(None),) * (m + 1) + (cols(c),)], dbuf.at[c % 2], dsem.at[c % 2]
        )

    def update_store(c):
        return pltpu.make_async_copy(ubuf.at[c % 2], u_ref.at[:, cols(c)], usem.at[c % 2])

    def back(c):
        gathered_load(c).wait()

        @pl.when(c >= 2)
        def _():
            update_store(c - 2).wait()

        tile = min(256, rows_here)
        direction = dbuf.at[c % 2]

        @pl.loop(0, rows_here // tile)
        def _(i):
            rows = pl.ds(pl.multiple_of(i * tile, tile), tile)
            product = jnp.dot(
                p_ref[rows, :],
                direction[...].reshape(rank, w),
                preferred_element_type=jnp.float32,
            )
            ubuf[c % 2, rows, :] = product.astype(ubuf.dtype)

        update_store(c).start()

    last = 2 * m
    lags = [0] + [LEAD + STRIDE * s for s in range(1, last + 1)]
    lags.append(lags[last] + 1)
    turn = list(range(last, 0, -1)) + [last + 1, 0]

    def step(c, s):
        if s == last + 1:

            @pl.when((c >= 0) & (c < chunks))
            def _():
                back(c)

            return
        for kind, order in enumerate(orders(m)):

            @pl.when((c >= 0) & (c < chunks) & ((c % 4 == 3) == (kind == 1)))
            def _():
                if 0 < s <= m:
                    rs_copy(c, s - 1, order).wait_recv()
                if s == 0:
                    project(c)
                elif s < m:
                    add(c, s - 1, order)
                elif s == m:
                    adam(c)
                    own_copy(c).start()
                else:
                    ag_copy(c, s - m - 1, order).wait_recv()
                    if s == m + 1:
                        own_copy(c).wait()
                    if s == last:
                        gathered_load(c).start()
                if s < m:
                    rs_copy(c, s, order).start()
                elif s < last:
                    ag_copy(c, s - m, order).start()

    def square_copy(i):
        return pltpu.make_async_remote_copy(
            src_ref=acc.at[i],
            dst_ref=slots.at[i],
            send_sem=sq_send.at[i],
            recv_sem=sq_recv.at[i],
            device_id=everyone[i],
            device_id_type=MESH,
        )

    def square_step(i):
        square_copy(i).wait_recv()
        acc[i + 1] = acc[i] + slots[i]
        if i + 1 < len(everyone):
            square_copy(i + 1).start()

    done = chunks + lags[m]

    @pl.loop(0, done)
    def _(t):
        for s in turn:
            step(t - lags[s], s)

    square_copy(0).start()
    for i in range(len(everyone)):
        square_step(i)
        if i < m:
            for s in turn:
                if s > m:
                    step(jnp.int32(done + i - lags[s]), s)

    @pl.loop(done + min(m, len(everyone)), chunks + lags[last + 1])
    def _(t):
        for s in turn:
            if s > m:
                step(t - lags[s], s)

    for c in range(max(chunks - 2, 0), chunks):
        update_store(c).wait()
    sq_ref[...] = acc[len(everyone)]

    for i in range(len(everyone)):
        square_copy(i).wait_send()

    @pl.loop(0, chunks)
    def _(c):
        for kind, order in enumerate(orders(m)):

            @pl.when((c % 4 == 3) == (kind == 1))
            def _():
                for j in range(m):
                    rs_copy(c, j, order).wait_send()
                    ag_copy(c, j, order).wait_send()


def local(n_row, n_col, gradient, projector, first_moment, second_moment):
    m, mc = log2(n_row), log2(n_col)
    rows, width = gradient.shape
    rank = projector.shape[1]
    chunks = chunks_of(width)
    rb, w = rank // n_row, width // chunks
    bf16, f32 = jnp.bfloat16, jnp.float32
    pairs = (2,) * m
    whole = pl.BlockSpec(memory_space=pltpu.VMEM)
    hbm = pl.BlockSpec(memory_space=pl.ANY)
    links = m + mc
    _, first_new, second_new, squares, unscaled = pl.pallas_call(
        functools.partial(kernel, n_row, n_col, chunks),
        out_shape=[
            jax.ShapeDtypeStruct(pairs + (rb, width), bf16),
            jax.ShapeDtypeStruct((rb, width), f32),
            jax.ShapeDtypeStruct((rb, width), f32),
            jax.ShapeDtypeStruct((8, 128), f32),
            jax.ShapeDtypeStruct((rows, width), bf16),
        ],
        in_specs=[whole, hbm, whole, whole],
        out_specs=[hbm, whole, whole, whole, hbm],
        scratch_shapes=[
            pltpu.VMEM((chunks,) + pairs + (rb, w), bf16),
            pltpu.VMEM((2, rows, w), bf16),
            pltpu.VMEM((chunks, rb, w), bf16),
            pltpu.VMEM((links + 1, 8, 128), f32),
            pltpu.VMEM((links, 8, 128), f32),
            pltpu.VMEM((rank, rows), bf16),
            pltpu.VMEM((2,) + pairs + (rb, w), bf16),
            pltpu.VMEM((2, rows, w), bf16),
        ]
        + [pltpu.VMEM((chunks,) + pairs[j + 1 :] + (rb, w), bf16) for j in range(m)]
        + [pltpu.SemaphoreType.DMA((2,))] * 3
        + [pltpu.SemaphoreType.DMA((m, chunks))] * 4
        + [pltpu.SemaphoreType.DMA((chunks,))]
        + [pltpu.SemaphoreType.DMA((links,))] * 2,
        cost_estimate=pl.CostEstimate(
            flops=4 * rows * rank * width,
            bytes_accessed=2 * rows * width + 2 * rank * width + 16 * rb * width,
            transcendentals=rb * width,
        ),
        compiler_params=pltpu.CompilerParams(
            collective_id=0, has_side_effects=True, vmem_limit_bytes=VMEM_BYTES
        ),
    )(projector, gradient, first_moment, second_moment)
    return scale(rank * width * n_col, unscaled, squares, first_new, second_new)


def scale_kernel(entries, v_ref, sq_ref, f_ref, s_ref, u_ref, fo_ref, so_ref):
    root_mean = jnp.sqrt(jnp.sum(sq_ref[...], keepdims=True) / entries + 1e-06)
    factor = jnp.minimum(1.0, clip_limit / root_mean)
    u_ref[...] = (v_ref[...].astype(jnp.float32) * factor).astype(u_ref.dtype)
    fo_ref[...] = f_ref[...]
    so_ref[...] = s_ref[...]


def scale(entries, unscaled, squares, first_new, second_new):
    rows, width = unscaled.shape
    rb = first_new.shape[0]
    steps = next(k for k in (8, 4, 2, 1) if rows % (16 * k) == 0 and rb % (8 * k) == 0 or k == 1)

    def down(height):
        return pl.BlockSpec((height // steps, width), lambda i: (i, 0))

    return pl.pallas_call(
        functools.partial(scale_kernel, entries),
        grid=(steps,),
        out_shape=[
            jax.ShapeDtypeStruct((rows, width), jnp.bfloat16),
            jax.ShapeDtypeStruct((rb, width), jnp.float32),
            jax.ShapeDtypeStruct((rb, width), jnp.float32),
        ],
        in_specs=[down(rows), pl.BlockSpec((8, 128), lambda i: (0, 0)), down(rb), down(rb)],
        out_specs=[down(rows), down(rb), down(rb)],
        compiler_params=pltpu.CompilerParams(vmem_limit_bytes=VMEM_BYTES),
    )(unscaled, squares, first_new, second_new)


def solution(mesh):
    placed = (P("row", "col"), P("row", None), P("row", "col"), P("row", "col"))
    return jax.shard_map(
        functools.partial(local, mesh.shape["row"], mesh.shape["col"]),
        mesh=mesh,
        in_specs=placed,
        out_specs=(P("row", "col"), P("row", "col"), P("row", "col")),
        check_vma=False,
    )
```

```python
import functools
import itertools

import jax
import jax.numpy as jnp
from jax import lax
from jax.experimental import pallas as pl
from jax.experimental.pallas import tpu as pltpu
from jax.sharding import PartitionSpec as P

MESH = pl.DeviceIdType.MESH

decay_first = 0.9
decay_second = 0.999
bias_first = 1.0 - 0.9**10
bias_second = 1.0 - 0.999**10
epsilon = 1e-08
clip_limit = 0.5

LEAD = 2
STRIDE = 3
VMEM_BYTES = 60 * 1024 * 1024


def chunks_of(width):
    return next(k for k in (28, 14, 8, 7, 4, 2, 1) if width % (128 * k) == 0 or k == 1)


def log2(count):
    return count.bit_length() - 1


def orders(m):
    plain = tuple(range(m))
    if m < 2:
        return plain, plain
    return plain, (1, 0) + plain[2:]


def kernel(n_row, n_col, chunks, p_ref, g_ref, m1_hbm, m2_hbm, *rest):
    m, mc = log2(n_row), log2(n_col)
    gath, f_hbm, s_hbm, sq_ref, u_ref, part, gbuf, dirv, acc, slots, pt_ref, dbuf, ubuf = rest[:13]
    m1_ref, m2_ref, f_ref, s_ref = rest[13:17]
    recvs = rest[17 : 17 + m]
    gsem, dsem, usem, msem, fsem, rs_send, rs_recv = rest[17 + m : 24 + m]
    ag_send, ag_recv, loc, sq_send, sq_recv = rest[24 + m :]
    rb, w = part.shape[-2:]
    rows_here, rank = p_ref.shape

    def bits_of(axis, count):
        me = lax.axis_index(axis)
        mine = [(me // (1 << b)) % 2 for b in range(count)]
        return mine, [{axis: me + (1 << b) * (1 - 2 * mine[b])} for b in range(count)]

    mine, partner = bits_of("row", m)
    _, col_partner = bits_of("col", mc)
    everyone = partner + col_partner

    def cols(c):
        return pl.ds(pl.multiple_of(c * w, w), w)

    def load(c):
        return pltpu.make_async_copy(g_ref.at[:, cols(c)], gbuf.at[c % 2], gsem.at[c % 2])

    barrier = pltpu.get_barrier_semaphore()
    for device in everyone:
        pl.semaphore_signal(barrier, inc=1, device_id=device, device_id_type=MESH)
    load(0).start()
    moments = [
        pltpu.make_async_copy(m1_hbm, m1_ref, msem.at[0]),
        pltpu.make_async_copy(m2_hbm, m2_ref, msem.at[1]),
    ]
    for copy in moments:
        copy.start()
    for r in range(0, rank, min(256, rank)):
        pt_ref[r : r + min(256, rank), :] = p_ref[:, r : r + min(256, rank)].T
    pl.semaphore_wait(barrier, len(everyone))
    for copy in moments:
        copy.wait()
    acc[0] = jnp.zeros(acc.shape[1:], acc.dtype)

    def index(fixed):
        return tuple(fixed.get(b, slice(None)) for b in reversed(range(m)))

    def rs_copy(c, j, order):
        fixed = {b: mine[b] for b in order[:j]}
        fixed[order[j]] = 1 - mine[order[j]]
        return pltpu.make_async_remote_copy(
            src_ref=part.at[(c,) + index(fixed)],
            dst_ref=recvs[j].at[c],
            send_sem=rs_send.at[j, c],
            recv_sem=rs_recv.at[j, c],
            device_id=partner[order[j]],
            device_id_type=MESH,
        )

    def ag_copy(c, j, order):
        fixed = {b: mine[b] for b in order[: m - j]}
        view = gath.at[(c,) + index(fixed)]
        return pltpu.make_async_remote_copy(
            src_ref=dirv.at[c] if j == 0 else view,
            dst_ref=view,
            send_sem=ag_send.at[j, c],
            recv_sem=ag_recv.at[j, c],
            device_id=partner[order[m - 1 - j]],
            device_id_type=MESH,
        )

    def own_copy(c):
        view = gath.at[(c,) + index(dict(enumerate(mine)))]
        return pltpu.make_async_copy(dirv.at[c], view, loc.at[c])

    def project(c):
        @pl.when(c + 1 < chunks)
        def _():
            load(c + 1).start()

        load(c).wait()
        tile = min(256, rank)
        per = tile // rb

        @pl.loop(0, rank // tile)
        def _(i):
            rows = pl.ds(pl.multiple_of(i * tile, tile), tile)
            product = jnp.dot(pt_ref[rows, :], gbuf[c % 2], preferred_element_type=jnp.float32)
            product = product.astype(part.dtype)
            for k in range(per):
                owner = i * per + k
                where = tuple((owner // (1 << b)) % 2 for b in reversed(range(m)))
                part[(c,) + where] = product[k * rb : (k + 1) * rb]

    def add(c, j, order):
        fixed = {b: mine[b] for b in order[: j + 1]}
        free = [b for b in reversed(range(m)) if b not in fixed]
        for values in itertools.product(range(2), repeat=len(free)):
            at = (c,) + index({**fixed, **dict(zip(free, values))})
            arrived = recvs[j][(c,) + values].astype(jnp.float32)
            part[at] = (part[at].astype(jnp.float32) + arrived).astype(part.dtype)

    def adam(c):
        at = (c,) + index(dict(enumerate(mine)))
        step = min(32, rb)
        for r in range(0, rb, step):
            rows = pl.ds(r, step)
            low = part[at + (rows, slice(None))].astype(jnp.float32)
            low = low + recvs[m - 1][c, rows, :].astype(jnp.float32)
            first = decay_first * m1_ref[rows, cols(c)] + (1.0 - decay_first) * low
            second = decay_second * m2_ref[rows, cols(c)] + (1.0 - decay_second) * low * low
            f_ref[rows, cols(c)] = first
            s_ref[rows, cols(c)] = second
            direction = first / bias_first / (jnp.sqrt(second / bias_second) + epsilon)
            dirv[c, rows, :] = direction.astype(dirv.dtype)
            square = direction * direction
            total = square[0:8]
            for k in range(8, step, 8):
                total = total + square[k : k + 8]
            for k in range(0, w, 128):
                acc[0] += total[:, k : k + 128]

    def gathered_load(c):
        return pltpu.make_async_copy(gath.at[c], dbuf.at[c % 2], dsem.at[c % 2])

    def moment_stores(c):
        return [
            pltpu.make_async_copy(f_ref.at[:, cols(c)], f_hbm.at[:, cols(c)], fsem.at[0, c]),
            pltpu.make_async_copy(s_ref.at[:, cols(c)], s_hbm.at[:, cols(c)], fsem.at[1, c]),
        ]

    def update_store(c):
        return pltpu.make_async_copy(ubuf.at[c % 2], u_ref.at[:, cols(c)], usem.at[c % 2])

    def back(c):
        gathered_load(c).wait()

        @pl.when(c >= 2)
        def _():
            update_store(c - 2).wait()

        tile = min(256, rows_here)
        direction = dbuf.at[c % 2]

        @pl.loop(0, rows_here // tile)
        def _(i):
            rows = pl.ds(pl.multiple_of(i * tile, tile), tile)
            product = jnp.dot(
                p_ref[rows, :],
                direction[...].reshape(rank, w),
                preferred_element_type=jnp.float32,
            )
            ubuf[c % 2, rows, :] = product.astype(ubuf.dtype)

        update_store(c).start()

    last = 2 * m
    lags = [0] + [LEAD + STRIDE * s for s in range(1, last + 1)]
    lags.append(lags[last] + 1)
    turn = list(range(last, 0, -1)) + [last + 1, 0]

    def step(c, s):
        if s == last + 1:

            @pl.when((c >= 0) & (c < chunks))
            def _():
                back(c)

            return
        for kind, order in enumerate(orders(m)):

            @pl.when((c >= 0) & (c < chunks) & ((c % 4 == 3) == (kind == 1)))
            def _():
                if 0 < s <= m:
                    rs_copy(c, s - 1, order).wait_recv()
                if s == 0:
                    project(c)
                elif s < m:
                    add(c, s - 1, order)
                elif s == m:
                    adam(c)
                    own_copy(c).start()
                    for copy in moment_stores(c):
                        copy.start()
                else:
                    ag_copy(c, s - m - 1, order).wait_recv()
                    if s == m + 1:
                        own_copy(c).wait()
                    if s == last:
                        gathered_load(c).start()
                if s < m:
                    rs_copy(c, s, order).start()
                elif s < last:
                    ag_copy(c, s - m, order).start()

    def square_copy(i):
        return pltpu.make_async_remote_copy(
            src_ref=acc.at[i],
            dst_ref=slots.at[i],
            send_sem=sq_send.at[i],
            recv_sem=sq_recv.at[i],
            device_id=everyone[i],
            device_id_type=MESH,
        )

    def square_step(i):
        square_copy(i).wait_recv()
        acc[i + 1] = acc[i] + slots[i]
        if i + 1 < len(everyone):
            square_copy(i + 1).start()

    done = chunks + lags[m]

    @pl.loop(0, done)
    def _(t):
        for s in turn:
            step(t - lags[s], s)

    square_copy(0).start()
    for i in range(len(everyone)):
        square_step(i)
        if i < m:
            for s in turn:
                if s > m:
                    step(jnp.int32(done + i - lags[s]), s)

    @pl.loop(done + min(m, len(everyone)), chunks + lags[last + 1])
    def _(t):
        for s in turn:
            if s > m:
                step(t - lags[s], s)

    for c in range(max(chunks - 2, 0), chunks):
        update_store(c).wait()
    sq_ref[...] = acc[len(everyone)]

    for i in range(len(everyone)):
        square_copy(i).wait_send()

    @pl.loop(0, chunks)
    def _(c):
        for copy in moment_stores(c):
            copy.wait()
        for kind, order in enumerate(orders(m)):

            @pl.when((c % 4 == 3) == (kind == 1))
            def _():
                for j in range(m):
                    rs_copy(c, j, order).wait_send()
                    ag_copy(c, j, order).wait_send()


def local(n_row, n_col, gradient, projector, first_moment, second_moment):
    m, mc = log2(n_row), log2(n_col)
    rows, width = gradient.shape
    rank = projector.shape[1]
    chunks = chunks_of(width)
    rb, w = rank // n_row, width // chunks
    bf16, f32 = jnp.bfloat16, jnp.float32
    pairs = (2,) * m
    whole = pl.BlockSpec(memory_space=pltpu.VMEM)
    hbm = pl.BlockSpec(memory_space=pl.ANY)
    links = m + mc
    _, first_new, second_new, squares, unscaled = pl.pallas_call(
        functools.partial(kernel, n_row, n_col, chunks),
        out_shape=[
            jax.ShapeDtypeStruct((chunks,) + pairs + (rb, w), bf16),
            jax.ShapeDtypeStruct((rb, width), f32),
            jax.ShapeDtypeStruct((rb, width), f32),
            jax.ShapeDtypeStruct((8, 128), f32),
            jax.ShapeDtypeStruct((rows, width), bf16),
        ],
        in_specs=[whole, hbm, hbm, hbm],
        out_specs=[hbm, hbm, hbm, whole, hbm],
        scratch_shapes=[
            pltpu.VMEM((chunks,) + pairs + (rb, w), bf16),
            pltpu.VMEM((2, rows, w), bf16),
            pltpu.VMEM((chunks, rb, w), bf16),
            pltpu.VMEM((links + 1, 8, 128), f32),
            pltpu.VMEM((links, 8, 128), f32),
            pltpu.VMEM((rank, rows), bf16),
            pltpu.VMEM((2,) + pairs + (rb, w), bf16),
            pltpu.VMEM((2, rows, w), bf16),
        ]
        + [pltpu.VMEM((rb, width), f32)] * 4
        + [pltpu.VMEM((chunks,) + pairs[j + 1 :] + (rb, w), bf16) for j in range(m)]
        + [pltpu.SemaphoreType.DMA((2,))] * 4
        + [pltpu.SemaphoreType.DMA((2, chunks))]
        + [pltpu.SemaphoreType.DMA((m, chunks))] * 4
        + [pltpu.SemaphoreType.DMA((chunks,))]
        + [pltpu.SemaphoreType.DMA((links,))] * 2,
        cost_estimate=pl.CostEstimate(
            flops=4 * rows * rank * width,
            bytes_accessed=2 * rows * width + 2 * rank * width + 16 * rb * width,
            transcendentals=rb * width,
        ),
        compiler_params=pltpu.CompilerParams(
            collective_id=0, has_side_effects=True, vmem_limit_bytes=VMEM_BYTES
        ),
    )(projector, gradient, first_moment, second_moment)
    return scale(rank * width * n_col, unscaled, squares, first_new, second_new)


def scale_kernel(entries, v_ref, sq_ref, f_ref, s_ref, u_ref, fo_ref, so_ref):
    root_mean = jnp.sqrt(jnp.sum(sq_ref[...], keepdims=True) / entries + 1e-06)
    factor = jnp.minimum(1.0, clip_limit / root_mean)
    u_ref[...] = (v_ref[...].astype(jnp.float32) * factor).astype(u_ref.dtype)
    fo_ref[...] = f_ref[...]
    so_ref[...] = s_ref[...]


def scale(entries, unscaled, squares, first_new, second_new):
    rows, width = unscaled.shape
    rb = first_new.shape[0]
    steps = next(k for k in (8, 4, 2, 1) if rows % (16 * k) == 0 and rb % (8 * k) == 0 or k == 1)

    def down(height):
        return pl.BlockSpec((height // steps, width), lambda i: (i, 0))

    return pl.pallas_call(
        functools.partial(scale_kernel, entries),
        grid=(steps,),
        out_shape=[
            jax.ShapeDtypeStruct((rows, width), jnp.bfloat16),
            jax.ShapeDtypeStruct((rb, width), jnp.float32),
            jax.ShapeDtypeStruct((rb, width), jnp.float32),
        ],
        in_specs=[down(rows), pl.BlockSpec((8, 128), lambda i: (0, 0)), down(rb), down(rb)],
        out_specs=[down(rows), down(rb), down(rb)],
        compiler_params=pltpu.CompilerParams(vmem_limit_bytes=VMEM_BYTES),
    )(unscaled, squares, first_new, second_new)


def solution(mesh):
    placed = (P("row", "col"), P("row", None), P("row", "col"), P("row", "col"))
    return jax.shard_map(
        functools.partial(local, mesh.shape["row"], mesh.shape["col"]),
        mesh=mesh,
        in_specs=placed,
        out_specs=(P("row", "col"), P("row", "col"), P("row", "col")),
        check_vma=False,
    )
```

```python
import functools
import itertools

import jax
import jax.numpy as jnp
from jax import lax
from jax.experimental import pallas as pl
from jax.experimental.pallas import tpu as pltpu
from jax.sharding import PartitionSpec as P

MESH = pl.DeviceIdType.MESH

decay_first = 0.9
decay_second = 0.999
bias_first = 1.0 - 0.9**10
bias_second = 1.0 - 0.999**10
epsilon = 1e-08
clip_limit = 0.5

LEAD = 2
STRIDE = 3
VMEM_BYTES = 60 * 1024 * 1024


def chunks_of(width):
    return next(k for k in (28, 14, 8, 7, 4, 2, 1) if width % (128 * k) == 0 or k == 1)


def log2(count):
    return count.bit_length() - 1


def orders(m):
    plain = tuple(range(m))
    if m < 2:
        return plain, plain
    return plain, (1, 0) + plain[2:]


def kernel(n_row, n_col, chunks, p_ref, g_ref, m1_hbm, m2_hbm, *rest):
    m, mc = log2(n_row), log2(n_col)
    gath, f_hbm, s_hbm, sq_ref, u_ref, part, gbuf, dirv, acc, slots, pt_ref, dbuf, ubuf = rest[:13]
    m1_ref, m2_ref, f_ref, s_ref = rest[13:17]
    recvs = rest[17 : 17 + m]
    gsem, dsem, usem, msem, fsem, rs_send, rs_recv = rest[17 + m : 24 + m]
    ag_send, ag_recv, loc, sq_send, sq_recv = rest[24 + m :]
    rb, w = part.shape[-2:]
    rows_here, rank = p_ref.shape

    def bits_of(axis, count):
        me = lax.axis_index(axis)
        mine = [(me // (1 << b)) % 2 for b in range(count)]
        return mine, [{axis: me + (1 << b) * (1 - 2 * mine[b])} for b in range(count)]

    mine, partner = bits_of("row", m)
    _, col_partner = bits_of("col", mc)
    everyone = partner + col_partner

    def cols(c):
        return pl.ds(pl.multiple_of(c * w, w), w)

    def load(c):
        return pltpu.make_async_copy(g_ref.at[:, cols(c)], gbuf.at[c % 2], gsem.at[c % 2])

    barrier = pltpu.get_barrier_semaphore()
    for device in everyone:
        pl.semaphore_signal(barrier, inc=1, device_id=device, device_id_type=MESH)
    load(0).start()
    moments = [
        pltpu.make_async_copy(m1_hbm, m1_ref, msem.at[0]),
        pltpu.make_async_copy(m2_hbm, m2_ref, msem.at[1]),
    ]
    for copy in moments:
        copy.start()
    for r in range(0, rank, min(256, rank)):
        pt_ref[r : r + min(256, rank), :] = p_ref[:, r : r + min(256, rank)].T
    pl.semaphore_wait(barrier, len(everyone))
    for copy in moments:
        copy.wait()
    acc[0] = jnp.zeros(acc.shape[1:], acc.dtype)

    def index(fixed):
        return tuple(fixed.get(b, slice(None)) for b in reversed(range(m)))

    def rs_copy(c, j, order):
        fixed = {b: mine[b] for b in order[:j]}
        fixed[order[j]] = 1 - mine[order[j]]
        return pltpu.make_async_remote_copy(
            src_ref=part.at[(c,) + index(fixed)],
            dst_ref=recvs[j].at[c],
            send_sem=rs_send.at[j, c],
            recv_sem=rs_recv.at[j, c],
            device_id=partner[order[j]],
            device_id_type=MESH,
        )

    def ag_copy(c, j, order):
        fixed = {b: mine[b] for b in order[: m - j]}
        view = gath.at[(c,) + index(fixed)]
        return pltpu.make_async_remote_copy(
            src_ref=dirv.at[c] if j == 0 else view,
            dst_ref=view,
            send_sem=ag_send.at[j, c],
            recv_sem=ag_recv.at[j, c],
            device_id=partner[order[m - 1 - j]],
            device_id_type=MESH,
        )

    def own_copy(c):
        view = gath.at[(c,) + index(dict(enumerate(mine)))]
        return pltpu.make_async_copy(dirv.at[c], view, loc.at[c])

    def project(c):
        @pl.when(c + 1 < chunks)
        def _():
            load(c + 1).start()

        load(c).wait()
        tile = min(256, rank)
        per = tile // rb

        @pl.loop(0, rank // tile)
        def _(i):
            rows = pl.ds(pl.multiple_of(i * tile, tile), tile)
            product = jnp.dot(pt_ref[rows, :], gbuf[c % 2], preferred_element_type=jnp.float32)
            product = product.astype(part.dtype)
            for k in range(per):
                owner = i * per + k
                where = tuple((owner // (1 << b)) % 2 for b in reversed(range(m)))
                part[(c,) + where] = product[k * rb : (k + 1) * rb]

    def add(c, j, order):
        fixed = {b: mine[b] for b in order[: j + 1]}
        free = [b for b in reversed(range(m)) if b not in fixed]
        for values in itertools.product(range(2), repeat=len(free)):
            at = (c,) + index({**fixed, **dict(zip(free, values))})
            arrived = recvs[j][(c,) + values].astype(jnp.float32)
            part[at] = (part[at].astype(jnp.float32) + arrived).astype(part.dtype)

    def adam(c):
        at = (c,) + index(dict(enumerate(mine)))
        step = min(32, rb)
        for r in range(0, rb, step):
            rows = pl.ds(r, step)
            low = part[at + (rows, slice(None))].astype(jnp.float32)
            low = low + recvs[m - 1][c, rows, :].astype(jnp.float32)
            first = decay_first * m1_ref[rows, cols(c)] + (1.0 - decay_first) * low
            second = decay_second * m2_ref[rows, cols(c)] + (1.0 - decay_second) * low * low
            f_ref[rows, cols(c)] = first
            s_ref[rows, cols(c)] = second
            direction = first / bias_first / (jnp.sqrt(second / bias_second) + epsilon)
            dirv[c, rows, :] = direction.astype(dirv.dtype)
            square = direction * direction
            total = square[0:8]
            for k in range(8, step, 8):
                total = total + square[k : k + 8]
            for k in range(0, w, 128):
                acc[0] += total[:, k : k + 128]

    def gathered_load(c):
        return pltpu.make_async_copy(gath.at[c], dbuf.at[c % 2], dsem.at[c % 2])

    def moment_stores(c):
        return [
            pltpu.make_async_copy(f_ref.at[:, cols(c)], f_hbm.at[:, cols(c)], fsem.at[0, c]),
            pltpu.make_async_copy(s_ref.at[:, cols(c)], s_hbm.at[:, cols(c)], fsem.at[1, c]),
        ]

    def update_store(c):
        return pltpu.make_async_copy(ubuf.at[c % 2], u_ref.at[:, cols(c)], usem.at[c % 2])

    def back(c):
        gathered_load(c).wait()

        @pl.when(c >= 2)
        def _():
            update_store(c - 2).wait()

        tile = min(256, rows_here)
        direction = dbuf.at[c % 2]

        @pl.loop(0, rows_here // tile)
        def _(i):
            rows = pl.ds(pl.multiple_of(i * tile, tile), tile)
            product = jnp.dot(
                p_ref[rows, :],
                direction[...].reshape(rank, w),
                preferred_element_type=jnp.float32,
            )
            ubuf[c % 2, rows, :] = product.astype(ubuf.dtype)

        update_store(c).start()

    last = 2 * m
    lags = [0] + [LEAD + STRIDE * s for s in range(1, last + 1)]
    lags.append(lags[last] + 1)
    turn = list(range(last, 0, -1)) + [last + 1, 0]

    def step(c, s):
        if s == last + 1:

            @pl.when((c >= 0) & (c < chunks))
            def _():
                back(c)

            return
        for kind, order in enumerate(orders(m)):

            @pl.when((c >= 0) & (c < chunks) & ((c % 7 == 6) == (kind == 1)))
            def _():
                if 0 < s <= m:
                    rs_copy(c, s - 1, order).wait_recv()
                if s == 0:
                    project(c)
                elif s < m:
                    add(c, s - 1, order)
                elif s == m:
                    adam(c)
                    own_copy(c).start()
                    for copy in moment_stores(c):
                        copy.start()
                else:
                    ag_copy(c, s - m - 1, order).wait_recv()
                    if s == m + 1:
                        own_copy(c).wait()
                    if s == last:
                        gathered_load(c).start()
                if s < m:
                    rs_copy(c, s, order).start()
                elif s < last:
                    ag_copy(c, s - m, order).start()

    def square_copy(i):
        return pltpu.make_async_remote_copy(
            src_ref=acc.at[i],
            dst_ref=slots.at[i],
            send_sem=sq_send.at[i],
            recv_sem=sq_recv.at[i],
            device_id=everyone[i],
            device_id_type=MESH,
        )

    def square_step(i):
        square_copy(i).wait_recv()
        acc[i + 1] = acc[i] + slots[i]
        if i + 1 < len(everyone):
            square_copy(i + 1).start()

    done = chunks + lags[m]

    @pl.loop(0, done)
    def _(t):
        for s in turn:
            step(t - lags[s], s)

    square_copy(0).start()
    for i in range(len(everyone)):
        square_step(i)
        if i < m:
            for s in turn:
                if s > m:
                    step(jnp.int32(done + i - lags[s]), s)

    @pl.loop(done + min(m, len(everyone)), chunks + lags[last + 1])
    def _(t):
        for s in turn:
            if s > m:
                step(t - lags[s], s)

    for c in range(max(chunks - 2, 0), chunks):
        update_store(c).wait()
    sq_ref[...] = acc[len(everyone)]

    for i in range(len(everyone)):
        square_copy(i).wait_send()

    @pl.loop(0, chunks)
    def _(c):
        for copy in moment_stores(c):
            copy.wait()
        for kind, order in enumerate(orders(m)):

            @pl.when((c % 7 == 6) == (kind == 1))
            def _():
                for j in range(m):
                    rs_copy(c, j, order).wait_send()
                    ag_copy(c, j, order).wait_send()


def local(n_row, n_col, gradient, projector, first_moment, second_moment):
    m, mc = log2(n_row), log2(n_col)
    rows, width = gradient.shape
    rank = projector.shape[1]
    chunks = chunks_of(width)
    rb, w = rank // n_row, width // chunks
    bf16, f32 = jnp.bfloat16, jnp.float32
    pairs = (2,) * m
    whole = pl.BlockSpec(memory_space=pltpu.VMEM)
    hbm = pl.BlockSpec(memory_space=pl.ANY)
    links = m + mc
    _, first_new, second_new, squares, unscaled = pl.pallas_call(
        functools.partial(kernel, n_row, n_col, chunks),
        out_shape=[
            jax.ShapeDtypeStruct((chunks,) + pairs + (rb, w), bf16),
            jax.ShapeDtypeStruct((rb, width), f32),
            jax.ShapeDtypeStruct((rb, width), f32),
            jax.ShapeDtypeStruct((8, 128), f32),
            jax.ShapeDtypeStruct((rows, width), bf16),
        ],
        in_specs=[whole, hbm, hbm, hbm],
        out_specs=[hbm, hbm, hbm, whole, hbm],
        scratch_shapes=[
            pltpu.VMEM((chunks,) + pairs + (rb, w), bf16),
            pltpu.VMEM((2, rows, w), bf16),
            pltpu.VMEM((chunks, rb, w), bf16),
            pltpu.VMEM((links + 1, 8, 128), f32),
            pltpu.VMEM((links, 8, 128), f32),
            pltpu.VMEM((rank, rows), bf16),
            pltpu.VMEM((2,) + pairs + (rb, w), bf16),
            pltpu.VMEM((2, rows, w), bf16),
        ]
        + [pltpu.VMEM((rb, width), f32)] * 4
        + [pltpu.VMEM((chunks,) + pairs[j + 1 :] + (rb, w), bf16) for j in range(m)]
        + [pltpu.SemaphoreType.DMA((2,))] * 4
        + [pltpu.SemaphoreType.DMA((2, chunks))]
        + [pltpu.SemaphoreType.DMA((m, chunks))] * 4
        + [pltpu.SemaphoreType.DMA((chunks,))]
        + [pltpu.SemaphoreType.DMA((links,))] * 2,
        cost_estimate=pl.CostEstimate(
            flops=4 * rows * rank * width,
            bytes_accessed=2 * rows * width + 2 * rank * width + 16 * rb * width,
            transcendentals=rb * width,
        ),
        compiler_params=pltpu.CompilerParams(
            collective_id=0, has_side_effects=True, vmem_limit_bytes=VMEM_BYTES
        ),
    )(projector, gradient, first_moment, second_moment)
    return scale(rank * width * n_col, unscaled, squares, first_new, second_new)


def scale_kernel(entries, v_ref, sq_ref, f_ref, s_ref, u_ref, fo_ref, so_ref):
    root_mean = jnp.sqrt(jnp.sum(sq_ref[...], keepdims=True) / entries + 1e-06)
    factor = jnp.minimum(1.0, clip_limit / root_mean)
    u_ref[...] = (v_ref[...].astype(jnp.float32) * factor).astype(u_ref.dtype)
    fo_ref[...] = f_ref[...]
    so_ref[...] = s_ref[...]


def scale(entries, unscaled, squares, first_new, second_new):
    rows, width = unscaled.shape
    rb = first_new.shape[0]
    steps = next(k for k in (8, 4, 2, 1) if rows % (16 * k) == 0 and rb % (8 * k) == 0 or k == 1)

    def down(height):
        return pl.BlockSpec((height // steps, width), lambda i: (i, 0))

    return pl.pallas_call(
        functools.partial(scale_kernel, entries),
        grid=(steps,),
        out_shape=[
            jax.ShapeDtypeStruct((rows, width), jnp.bfloat16),
            jax.ShapeDtypeStruct((rb, width), jnp.float32),
            jax.ShapeDtypeStruct((rb, width), jnp.float32),
        ],
        in_specs=[down(rows), pl.BlockSpec((8, 128), lambda i: (0, 0)), down(rb), down(rb)],
        out_specs=[down(rows), down(rb), down(rb)],
        compiler_params=pltpu.CompilerParams(vmem_limit_bytes=VMEM_BYTES),
    )(unscaled, squares, first_new, second_new)


def solution(mesh):
    placed = (P("row", "col"), P("row", None), P("row", "col"), P("row", "col"))
    return jax.shard_map(
        functools.partial(local, mesh.shape["row"], mesh.shape["col"]),
        mesh=mesh,
        in_specs=placed,
        out_specs=(P("row", "col"), P("row", "col"), P("row", "col")),
        check_vma=False,
    )
```
